128 devices in a mesh: ctx: 16 (over z, y), fsdp: 8 (over x, core).
Axes of the slice: x: 4, y: 4, z: 4, core: 2. Of those that a mesh axis runs over, the one named last changes fastest.
Arguments:
- tokens: bfloat16 [24, 2048, 2048], P('fsdp', 'ctx'), may hold values from -6 to 6
- segment_ids: int32 [24, 2048], P('fsdp'), may hold values from 0 to 7, as said below
- end_rows: int32 [24, 8], P('fsdp'), may hold values from 0 to 2047, as said below
- input_norm_gain: float32 [2048], replicated, may hold values from 0.25 to 1.75
- query_weight: bfloat16 [2048, 1024], P(('ctx', 'fsdp')), may hold values from -1 to 1
- key_weight: bfloat16 [2048, 256], P(('ctx', 'fsdp')), may hold values from -1 to 1
- value_weight: bfloat16 [2048, 256], P(('ctx', 'fsdp')), may hold values from -0.125 to 0.125
- out_weight: bfloat16 [2048, 1024], P(('ctx', 'fsdp')), may hold values from -0.75 to 0.75
- head_weight: float32 [2048], replicated, may hold values from -0.125 to 0.125
- branch_grad: bfloat16 [24, 2048, 2048], P('fsdp', 'ctx'), may hold values from -6 to 6
Outputs:
- branch: bfloat16 [24, 2048, 2048], P('fsdp', 'ctx')
- rewards: float32 [24, 8], P('fsdp')
- grad_tokens: bfloat16 [24, 2048, 2048], P('fsdp', 'ctx')
- grad_query_weight: float32 [2048, 1024], P(('ctx', 'fsdp'))
- grad_key_weight: float32 [2048, 256], P(('ctx', 'fsdp'))
- grad_value_weight: float32 [2048, 256], P(('ctx', 'fsdp'))
- grad_out_weight: float32 [2048, 1024], P(('ctx', 'fsdp'))
The draws below stay inside these ranges and needn't reach their ends.
Inputs may be any that keep to these rules, and one draw needn't show every extreme that they name: `segment_ids`: never falling along a slab; document d holds the positions after end_rows of d - 1 up to end_rows of d. `end_rows`: strictly rising within a slab; the last is always 2048 - 1.
All inputs are finite; a program needn't handle non-finite values.
Results may differ from the reference program's by a relative error of at most 0.03.
The reference program's roundings to bfloat16 on the way count: a program that leaves them out, or rounds other values in their place, can miss the bound.
Values may be sent and summed in bfloat16 or wider, within the bound.
No kernel may reach another device: no remote copies, remote signals or barrier semaphores. Data moves between devices by JAX's collectives and lax.ppermute only.
A program may use at most 192 MiB of HBM per device.

```python
import jax
import jax.numpy as jnp
from jax import lax

D = 2048
HEADS = 16
KV_HEADS = 4
HEAD_DIM = 64
DOCS = 8
SLAB = 2048
SLABS = 24


def document_cuts(key):

    def one_slab(index):
        picks = jax.random.permutation(jax.random.fold_in(key, index), SLAB - 1)[:DOCS - 1] + 1
        return jnp.sort(picks).astype(jnp.int32)
    return jax.vmap(one_slab)(jnp.arange(SLABS, dtype=jnp.int32))


def draw_segment_ids(key, part):
    cuts = document_cuts(key)
    place = jnp.arange(SLAB, dtype=jnp.int32)
    return jnp.sum((place[None, :, None] >= cuts[:, None, :]).astype(jnp.int32), -1).astype(jnp.int32)


def draw_end_rows(key, part):
    cuts = document_cuts(key)
    last = jnp.full((SLABS, 1), SLAB - 1, jnp.int32)
    return jnp.concatenate([cuts - 1, last], 1).astype(jnp.int32)


def draw_query_weight(key, part):
    key = jax.random.fold_in(key, 5)
    fresh = jax.random.normal(key, (D, HEADS * HEAD_DIM), jnp.float32) * D ** (-0.5)
    return fresh.astype(jnp.bfloat16)


def draw_key_weight(key, part):
    key = jax.random.fold_in(key, 7)
    noise = jax.random.normal(key, (D, KV_HEADS * HEAD_DIM), jnp.float32) * D ** (-0.5)
    return noise.astype(jnp.bfloat16)


def spiked(entries, own_key, source, target, parts, factor):
    owner, partner = [(jnp.arange(entries.shape[axis_at]) // (entries.shape[axis_at] // parts)).reshape([-1 if axis == axis_at else 1 for axis in range(entries.ndim)]) for axis_at in (source, target)]
    chosen = jax.random.permutation(own_key, parts)[partner]
    strong = (owner == chosen) | (owner == (partner + parts // 2) % parts)
    return jnp.where(strong, factor * entries, entries)


def steps_of(stream_key, shape, split, smallest, largest):
    def one(dim, shards_of):
        draws = jax.random.uniform(jax.random.fold_in(jax.random.fold_in(stream_key, 6), dim), (shards_of,), jnp.float32, smallest / len(split), largest / len(split))
        return jnp.repeat(jnp.exp(draws), shape[dim] // shards_of).reshape((-1,) + (1,) * (len(shape) - dim - 1))

    gain = one(*split[0])
    for cut in split[1:]:
        gain = gain * one(*cut)
    return gain


def gaussian(stream_key, dims, scale, most, pieces=(), kind=jnp.bfloat16):
    gain = steps_of(stream_key, dims, pieces, -0.22, 0.18) if pieces else 1.0
    entries = jax.random.normal(stream_key, dims, jnp.float32) * scale * gain
    return jnp.minimum(jnp.maximum(entries, -most), most).astype(kind)


def bell_draw_with(stream_key, extent, scale, reach, shards, heavy, kind=jnp.bfloat16):
    drawn = scale * jax.random.normal(stream_key, extent, jnp.float32)
    if shards:
        drawn = drawn * steps_of(stream_key, extent, shards, -0.22, 0.18)
    return jnp.clip(spiked(drawn, jax.random.fold_in(stream_key, 3), *heavy), -reach, reach).astype(kind)


def setup_inputs(seed: int = 0) -> dict:
    arg_keys = jax.random.split(jax.random.key(seed), 11)
    tokens = gaussian(arg_keys[0], (SLABS, SLAB, D), 1.0, 6.0, ((0, 8), (1, 16)))
    segment_ids = draw_segment_ids(jax.random.fold_in(arg_keys[10], 71), 0)
    end_rows = draw_end_rows(jax.random.fold_in(arg_keys[10], 71), 0)
    input_norm_gain = jnp.clip(1.0 + 0.15 * jax.random.normal(arg_keys[3], (D,), jnp.float32), 0.25, 1.75)
    query_weight = draw_query_weight(jax.random.fold_in(arg_keys[10], 71), 0)
    key_weight = draw_key_weight(jax.random.fold_in(arg_keys[10], 71), 0)
    value_weight = gaussian(arg_keys[6], (D, KV_HEADS * HEAD_DIM), D ** -0.5, 0.125, ((0, 128),))
    out_weight = gaussian(arg_keys[7], (D, HEADS * HEAD_DIM), HEAD_DIM ** -0.5, 0.75, ((0, 128),))
    head_weight = gaussian(arg_keys[8], (D,), D ** -0.5, 0.125, (), jnp.float32)
    branch_grad = bell_draw_with(arg_keys[9], (SLABS, SLAB, D), 1.0, 6.0, ((0, 8), (1, 16)), (1, 2, 16, 2.0))
    return dict(tokens=tokens, segment_ids=segment_ids, end_rows=end_rows, input_norm_gain=input_norm_gain, query_weight=query_weight, key_weight=key_weight, value_weight=value_weight, out_weight=out_weight, head_weight=head_weight, branch_grad=branch_grad)


eps = 1e-05
base_theta = 500000.0

def rotation_tables(first, count):
    half = HEAD_DIM // 2
    freqs = base_theta ** (-(2.0 * jnp.arange(half, dtype=jnp.float32)) / HEAD_DIM)
    angles = (first + jnp.arange(count, dtype=jnp.int32)).astype(jnp.float32)[:, None] * freqs[None, :]
    return (jnp.cos(angles)[:, None, :], jnp.sin(angles)[:, None, :])

def rotate(values, cosine, sine):
    half = values.shape[-1] // 2
    front = values[..., :half]
    back = values[..., half:]
    return jnp.concatenate([front * cosine - back * sine, back * cosine + front * sine], -1)

def normalize(values):
    return values * lax.rsqrt(lax.optimization_barrier(jnp.mean(values * values, -1, keepdims=True)) + eps)

def heads_first(values):
    return jnp.swapaxes(values, 0, 1)

def one_slab(tokens, segments, ends, grad_out, gain_vector, wq, wk, wv, wo, head_weight):
    group = HEADS // KV_HEADS
    scale = HEAD_DIM ** (-0.5)
    width = HEADS * HEAD_DIM
    input_float = tokens.astype(jnp.float32)
    inverse_norm = lax.rsqrt(lax.optimization_barrier(jnp.mean(input_float * input_float, -1, keepdims=True)) + eps)
    centered_input = input_float * inverse_norm
    normalized_input = (centered_input * gain_vector).astype(jnp.bfloat16)
    cosine, sine = rotation_tables(0, SLAB)
    query = rotate(jnp.dot(normalized_input, wq, preferred_element_type=jnp.float32).reshape(SLAB, HEADS, HEAD_DIM), cosine, sine).astype(jnp.bfloat16)
    keys = rotate(jnp.dot(normalized_input, wk, preferred_element_type=jnp.float32).reshape(SLAB, KV_HEADS, HEAD_DIM), cosine, sine).astype(jnp.bfloat16)
    values = jnp.dot(normalized_input, wv, preferred_element_type=jnp.float32).astype(jnp.bfloat16).reshape(SLAB, KV_HEADS, HEAD_DIM)
    keys = jnp.repeat(keys, group, axis=1)
    values = jnp.repeat(values, group, axis=1)
    place = jnp.arange(SLAB, dtype=jnp.int32)
    allowed = (place[None, :] <= place[:, None]) & (segments[None, :] == segments[:, None])

    def probabilities(query_head, key_head):
        scores = jnp.dot(query_head, key_head.T, preferred_element_type=jnp.float32) * scale
        scores = jnp.where(allowed, scores, -jnp.inf)
        top = lax.optimization_barrier(jnp.max(scores, -1, keepdims=True))
        weights = jnp.exp(scores - top)
        return weights / lax.optimization_barrier(jnp.sum(weights, -1, keepdims=True))

    def forward_head(packed):
        query_head, key_head, value_head = packed
        probs_low = probabilities(query_head, key_head).astype(jnp.bfloat16)
        return jnp.dot(probs_low, value_head, preferred_element_type=jnp.float32).astype(jnp.bfloat16)
    context = lax.map(forward_head, (heads_first(query), heads_first(keys), heads_first(values)))
    context_rows = heads_first(context).reshape(SLAB, width)
    branch = jnp.dot(context_rows, wo.T, preferred_element_type=jnp.float32).astype(jnp.bfloat16)
    hidden = input_float + branch.astype(jnp.float32)
    picked = normalize(hidden[ends])
    rewards = lax.optimization_barrier(jnp.sum(picked * head_weight, -1))
    context_grad = jnp.dot(grad_out, wo, preferred_element_type=jnp.float32).astype(jnp.bfloat16).reshape(SLAB, HEADS, HEAD_DIM)

    def backward_head(packed):
        query_head, key_head, value_head, context_head, grad_head = packed
        probs = probabilities(query_head, key_head)
        dprobs = jnp.dot(grad_head, value_head.T, preferred_element_type=jnp.float32)
        delta = lax.optimization_barrier(jnp.sum(grad_head.astype(jnp.float32) * context_head.astype(jnp.float32), -1, keepdims=True))
        dscores = (probs * (dprobs - delta)).astype(jnp.bfloat16)
        dq = jnp.dot(dscores, key_head, preferred_element_type=jnp.float32) * scale
        dk = jnp.dot(dscores.T, query_head, preferred_element_type=jnp.float32) * scale
        dv = jnp.dot(probs.astype(jnp.bfloat16).T, grad_head, preferred_element_type=jnp.float32)
        return (dq, dk, dv)
    dq, dk, dv = lax.map(backward_head, (heads_first(query), heads_first(keys), heads_first(values), context, heads_first(context_grad)))
    dquery = rotate(heads_first(dq), cosine, -sine).astype(jnp.bfloat16).reshape(SLAB, width)
    dkey_head = rotate(heads_first(dk), cosine, -sine).astype(jnp.bfloat16)
    dvalue_head = heads_first(dv).astype(jnp.bfloat16)
    dkey = lax.optimization_barrier(jnp.sum(dkey_head.astype(jnp.float32).reshape(SLAB, KV_HEADS, group, HEAD_DIM), 2)).astype(jnp.bfloat16).reshape(SLAB, KV_HEADS * HEAD_DIM)
    dvalue = lax.optimization_barrier(jnp.sum(dvalue_head.astype(jnp.float32).reshape(SLAB, KV_HEADS, group, HEAD_DIM), 2)).astype(jnp.bfloat16).reshape(SLAB, KV_HEADS * HEAD_DIM)
    grad_q = jnp.dot(normalized_input.T, dquery, preferred_element_type=jnp.float32)
    grad_k = jnp.dot(normalized_input.T, dkey, preferred_element_type=jnp.float32)
    grad_v = jnp.dot(normalized_input.T, dvalue, preferred_element_type=jnp.float32)
    grad_o = jnp.dot(grad_out.T, context_rows, preferred_element_type=jnp.float32)
    dnormed = jnp.dot(dquery, wq.T, preferred_element_type=jnp.float32)
    dnormed = dnormed + jnp.dot(dkey, wk.T, preferred_element_type=jnp.float32)
    dnormed = dnormed + jnp.dot(dvalue, wv.T, preferred_element_type=jnp.float32)
    scaled_input = dnormed * gain_vector
    input_gradient = (inverse_norm * (scaled_input - centered_input * lax.optimization_barrier(jnp.mean(scaled_input * centered_input, -1, keepdims=True)))).astype(jnp.bfloat16)
    return (branch, rewards, input_gradient, grad_q, grad_k, grad_v, grad_o)

def reference(tokens, segment_ids, end_rows, input_norm_gain, query_weight, key_weight, value_weight, out_weight, head_weight, branch_grad):

    def per_slab(packed):
        return one_slab(packed[0], packed[1], packed[2], packed[3], input_norm_gain, query_weight, key_weight, value_weight, out_weight, head_weight)
    branch, rewards, input_gradient, grad_q, grad_k, grad_v, grad_o = lax.map(per_slab, (tokens, segment_ids, end_rows, branch_grad))
    return (branch, rewards, input_gradient, lax.optimization_barrier(jnp.sum(grad_q, 0)), lax.optimization_barrier(jnp.sum(grad_k, 0)), lax.optimization_barrier(jnp.sum(grad_v, 0)), lax.optimization_barrier(jnp.sum(grad_o, 0)))
```

```python
import jax
import jax.numpy as jnp
from jax import lax
from jax.experimental import pallas as pl
from jax.experimental.pallas import tpu as pltpu
from jax.sharding import Mesh
from jax.sharding import PartitionSpec as P

HEADS = 16
KV_HEADS = 4
HEAD_DIM = 64
GROUP = HEADS // KV_HEADS
HALF = HEAD_DIM // 2
BLOCK = 256

eps = 1e-05
base_theta = 500000.0


def rotation_tables(positions):
    freqs = base_theta ** (-(2.0 * jnp.arange(HALF, dtype=jnp.float32)) / HEAD_DIM)
    angles = positions.astype(jnp.float32)[None, :] * freqs[:, None]
    return jnp.cos(angles), jnp.sin(angles)


def attention_kernel(
    ends_ref, in_ref, cos_ref, sin_ref, out_ref, kt_s, k_s, vt_s, v_s, p_s, dk_s, dv_s
):
    slab = pl.program_id(0)
    n_src, _, rows = in_ref.shape
    per = BLOCK // rows
    blocks = n_src // per
    docs = ends_ref.shape[1]
    f32, bf16 = jnp.float32, jnp.bfloat16
    hd = HEAD_DIM

    def load(b, part):
        return jnp.concatenate(
            [in_ref[b * per + r, part * hd : (part + 1) * hd, :] for r in range(per)], axis=1
        )

    for b in range(blocks):
        kt = load(b, 1)
        vt = load(b, 2)
        kt_s[b] = kt
        vt_s[b] = vt
        k_s[b] = kt.T
        v_s[b] = vt.T
    dk_s[...] = jnp.zeros_like(dk_s)
    dv_s[...] = jnp.zeros_like(dv_s)

    key_iota = lax.broadcasted_iota(jnp.int32, (BLOCK, BLOCK), 0)
    row_iota = lax.broadcasted_iota(jnp.int32, (1, BLOCK), 1)

    for i in range(blocks):
        qt = load(i, 0)
        dot_t = load(i, 3)
        place = row_iota + i * BLOCK
        start = jnp.zeros((1, BLOCK), jnp.int32)
        first = jnp.int32(0)
        for d in range(docs - 1):
            after = ends_ref[slab, d] + 1
            start = jnp.where(place >= after, after, start)
            first = jnp.where(after <= i * BLOCK, after, first)
        lo = lax.shift_right_logical(first, BLOCK.bit_length() - 1)

        def scores(j, top, qt=qt, place=place, start=start):
            s = jnp.dot(k_s[j], qt, preferred_element_type=f32)
            at = key_iota + j * BLOCK
            s = jnp.where((at >= start) & (at <= place), s, -jnp.inf)
            p_s[j] = s
            return jnp.maximum(top, jnp.max(s, axis=0, keepdims=True))

        top = scores(i, jnp.full((1, BLOCK), -jnp.inf, f32))
        top = lax.fori_loop(lo, i, scores, top)

        def forward(j, carry, top=top):
            total, acc = carry
            w = jnp.exp(p_s[j] - top)
            p_s[j] = w
            total = total + jnp.sum(w, axis=0, keepdims=True)
            acc = acc + jnp.dot(vt_s[j], w.astype(bf16), preferred_element_type=f32)
            return total, acc

        carry = forward(i, (jnp.zeros((1, BLOCK), f32), jnp.zeros((hd, BLOCK), f32)))
        total, acc = lax.fori_loop(lo, i, forward, carry)
        inv = 1.0 / total
        ctx = (acc * inv).astype(bf16)
        delta = jnp.sum(dot_t.astype(f32) * ctx.astype(f32), axis=0, keepdims=True)

        def backward(j, dq, qt=qt, dot_t=dot_t, inv=inv, delta=delta):
            probs = p_s[j] * inv
            dp = jnp.dot(v_s[j], dot_t, preferred_element_type=f32)
            ds = (probs * (dp - delta)).astype(bf16)
            trans = (((1,), (1,)), ((), ()))
            dv_s[j] += lax.dot_general(
                dot_t, probs.astype(bf16), trans, preferred_element_type=f32
            )
            dk_s[j] += lax.dot_general(qt, ds, trans, preferred_element_type=f32)
            return dq + jnp.dot(kt_s[j], ds, preferred_element_type=f32)

        dq = backward(i, jnp.zeros((hd, BLOCK), f32))
        dq = lax.fori_loop(lo, i, backward, dq) * (hd**-0.5)
        for r in range(per):
            at = slice(r * rows, (r + 1) * rows)
            src = i * per + r
            out_ref[src, 0:hd, :] = ctx[:, at]
            a, b = dq[:HALF, at], dq[HALF:, at]
            cosine, sine = cos_ref[src], sin_ref[src]
            out_ref[src, hd : hd + HALF, :] = (a * cosine + b * sine).astype(bf16)
            out_ref[src, hd + HALF : 2 * hd, :] = (b * cosine - a * sine).astype(bf16)

    for j in range(blocks):
        for r in range(per):
            at = slice(r * rows, (r + 1) * rows)
            src = j * per + r
            a, b = dk_s[j, :HALF, at], dk_s[j, HALF:, at]
            cosine, sine = cos_ref[src], sin_ref[src]
            out_ref[src, 2 * hd : 2 * hd + HALF, :] = (a * cosine + b * sine).astype(bf16)
            out_ref[src, 2 * hd + HALF : 3 * hd, :] = (b * cosine - a * sine).astype(bf16)
            out_ref[src, 3 * hd : 4 * hd, :] = dv_s[j, :, at].astype(bf16)


def attention(received, ends, cos_all, sin_all):
    n_src, width, tok = received.shape
    slabs = ends.shape[0]
    rows = tok // slabs
    blocks = n_src * rows // BLOCK
    bf16, f32 = jnp.bfloat16, jnp.float32
    table = pl.BlockSpec((n_src, HALF, rows), lambda s, e: (0, 0, 0))
    part = pl.BlockSpec((n_src, width, rows), lambda s, e: (0, 0, s))
    return pl.pallas_call(
        attention_kernel,
        out_shape=jax.ShapeDtypeStruct(received.shape, bf16),
        grid_spec=pltpu.PrefetchScalarGridSpec(
            num_scalar_prefetch=1,
            grid=(slabs,),
            in_specs=[part, table, table],
            out_specs=part,
            scratch_shapes=[
                pltpu.VMEM((blocks, HEAD_DIM, BLOCK), bf16),
                pltpu.VMEM((blocks, BLOCK, HEAD_DIM), bf16),
                pltpu.VMEM((blocks, HEAD_DIM, BLOCK), bf16),
                pltpu.VMEM((blocks, BLOCK, HEAD_DIM), bf16),
                pltpu.VMEM((blocks, BLOCK, BLOCK), f32),
                pltpu.VMEM((blocks, HEAD_DIM, BLOCK), f32),
                pltpu.VMEM((blocks, HEAD_DIM, BLOCK), f32),
            ],
        ),
        compiler_params=pltpu.CompilerParams(vmem_limit_bytes=40 * 1024 * 1024),
        cost_estimate=pl.CostEstimate(
            flops=20 * 10**9, bytes_accessed=6 * 2**20, transcendentals=3 * 2**20
        ),
        name="attention",
    )(ends, received, cos_all, sin_all)


def on_device(
    tokens,
    segment_ids,
    end_rows,
    input_norm_gain,
    query_weight,
    key_weight,
    value_weight,
    out_weight,
    head_weight,
    branch_grad,
):
    del segment_ids
    bf16, f32 = jnp.bfloat16, jnp.float32
    n_ctx, n_x, n_core = (lax.axis_size(a) for a in ("ctx", "x", "core"))
    rank = lax.axis_index("ctx")
    core = lax.axis_index("core")
    slabs, rows, model = tokens.shape
    docs = end_rows.shape[1]
    tok = slabs * rows
    width = HEADS * HEAD_DIM
    kv_width = KV_HEADS * HEAD_DIM
    qkv = width + 2 * kv_width
    swap = [(c, n_core - 1 - c) for c in range(n_core)]

    weights = lax.all_gather(
        jnp.concatenate([query_weight, key_weight, value_weight, out_weight], 1),
        ("ctx", "x", "core"),
        axis=0,
        tiled=True,
    )

    flat = tokens.reshape(tok, model)
    grad_out = branch_grad.reshape(tok, model)
    wide = flat.astype(f32)
    inverse_norm = lax.rsqrt(jnp.mean(wide * wide, -1, keepdims=True) + eps)
    normed = (wide * inverse_norm * input_norm_gain).astype(bf16)

    def by_core(values):
        split = values.T.reshape(model // (16 * n_core), n_core, 16, tok)
        mine = lax.dynamic_index_in_dim(split, core, 1, keepdims=False).reshape(-1, tok)
        other = lax.dynamic_index_in_dim(split, 1 - core, 1, keepdims=False).reshape(-1, tok)
        return mine, lax.ppermute(other, "core", swap)

    normed_mine, normed_other = by_core(normed)
    grad_out_mine, grad_out_other = by_core(grad_out)

    first = rank * rows
    cos_all, sin_all = rotation_tables(jnp.arange(n_ctx * rows, dtype=jnp.int32))
    cos_here, sin_here = rotation_tables(first + jnp.arange(rows, dtype=jnp.int32))
    cos_here = jnp.tile(cos_here, (1, slabs))[None]
    sin_here = jnp.tile(sin_here, (1, slabs))[None]
    over = (((0,), (1,)), ((), ()))
    projected = lax.dot_general(weights[:, :qkv], normed, over, preferred_element_type=f32)
    turning = projected[: width + kv_width].reshape(HEADS + KV_HEADS, 2, HALF, tok)
    front, back = turning[:, 0], turning[:, 1]
    turned = jnp.concatenate(
        [front * cos_here - back * sin_here, back * cos_here + front * sin_here], 1
    )
    query = (turned[:HEADS] * (HEAD_DIM**-0.5)).astype(bf16)
    keys = jnp.repeat(turned[HEADS:].astype(bf16), GROUP, axis=0)
    values = projected[width + kv_width :].astype(bf16).reshape(KV_HEADS, HEAD_DIM, tok)
    values = jnp.repeat(values, GROUP, axis=0)
    context_grad = lax.dot_general(
        weights[:, qkv:], grad_out, over, preferred_element_type=f32
    ).astype(bf16)
    send = jnp.concatenate(
        [query, keys, values, context_grad.reshape(HEADS, HEAD_DIM, tok)], 1
    )
    received = lax.all_to_all(send, "ctx", split_axis=0, concat_axis=0, tiled=True)

    def by_source(table):
        return jnp.swapaxes(table.reshape(HALF, n_ctx, rows), 0, 1)

    results = attention(received, end_rows, by_source(cos_all), by_source(sin_all))
    back_home = lax.all_to_all(results, "ctx", split_axis=0, concat_axis=0, tiled=True)

    hd = HEAD_DIM
    context = back_home[:, :hd].reshape(width, tok)
    dquery = back_home[:, hd : 2 * hd].reshape(width, tok)

    def over_group(heads):
        heads = heads.astype(f32).reshape(KV_HEADS, GROUP, hd, tok)
        return jnp.sum(heads, 1).astype(bf16).reshape(kv_width, tok)

    dkey = over_group(back_home[:, 2 * hd : 3 * hd])
    dvalue = over_group(back_home[:, 3 * hd :])
    grads = jnp.concatenate([dquery, dkey, dvalue], 0)
    sent = lax.ppermute(jnp.concatenate([grads, context], 0), "core", swap)

    last = (((1,), (1,)), ((), ()))

    def two(a, b, c, d):
        return lax.dot_general(
            jnp.concatenate([a, c], 1),
            jnp.concatenate([b, d], 1),
            last,
            preferred_element_type=f32,
        ).astype(bf16)

    partial = jnp.concatenate(
        [
            two(normed_mine, grads, normed_other, sent[:qkv]),
            two(grad_out_mine, context, grad_out_other, sent[qkv:]),
        ],
        1,
    )
    summed = lax.psum_scatter(partial, "ctx", scatter_dimension=0, tiled=True)
    pieces = lax.all_to_all(summed, "x", split_axis=0, concat_axis=0, tiled=True)
    summed = jnp.sum(pieces.astype(f32).reshape(n_x, -1, qkv + width), 0)

    branch = lax.dot_general(context, weights[:, qkv:], over, preferred_element_type=f32)
    branch = branch.astype(bf16)
    here = jnp.arange(slabs, dtype=jnp.int32)
    marks = (
        (end_rows[:, :, None, None] == first + jnp.arange(rows, dtype=jnp.int32))
        & (here[:, None, None, None] == here[:, None])
    ).astype(bf16)
    marks = marks.reshape(slabs * docs, tok)
    picked = jnp.dot(marks, flat, preferred_element_type=f32) + jnp.dot(
        marks, branch, preferred_element_type=f32
    )
    picked = picked * lax.rsqrt(jnp.mean(picked * picked, -1, keepdims=True) + eps)
    rewards = jnp.sum(picked * head_weight, -1).reshape(slabs, docs)
    step = 1
    while step < n_ctx:
        pairs = [(c, c ^ step) for c in range(n_ctx)]
        rewards = rewards + lax.ppermute(rewards, "ctx", pairs)
        step *= 2

    dnormed = lax.dot_general(grads, weights[:, :qkv], over, preferred_element_type=f32)
    scaled = dnormed * input_norm_gain
    centered = wide * inverse_norm
    grad_tokens = inverse_norm * (
        scaled - centered * jnp.mean(scaled * centered, -1, keepdims=True)
    )
    return (
        branch.reshape(tokens.shape),
        rewards,
        grad_tokens.astype(bf16).reshape(tokens.shape),
        summed[:, :width],
        summed[:, width : width + kv_width],
        summed[:, width + kv_width : qkv],
        summed[:, qkv:],
    )


def solution(mesh):
    n_ctx, n_fsdp = mesh.devices.shape
    chips = Mesh(mesh.devices.reshape(n_ctx, n_fsdp // 2, 2), ("ctx", "x", "core"))
    fsdp = ("x", "core")
    rows = P(("ctx", "x", "core"), None)
    acts = P(fsdp, "ctx", None)
    return jax.shard_map(
        on_device,
        mesh=chips,
        in_specs=(
            acts,
            P(fsdp, None),
            P(fsdp, None),
            P(),
            rows,
            rows,
            rows,
            rows,
            P(),
            acts,
        ),
        out_specs=(acts, P(fsdp, None), acts, rows, rows, rows, rows),
        check_vma=False,
    )
```

```python
import jax
import jax.numpy as jnp
from jax import lax
from jax.experimental import pallas as pl
from jax.experimental.pallas import tpu as pltpu
from jax.sharding import Mesh
from jax.sharding import PartitionSpec as P

HEADS = 16
KV_HEADS = 4
HEAD_DIM = 64
GROUP = HEADS // KV_HEADS
HALF = HEAD_DIM // 2
BLOCK = 256

eps = 1e-05
base_theta = 500000.0


def rotation_tables(positions):
    freqs = base_theta ** (-(2.0 * jnp.arange(HALF, dtype=jnp.float32)) / HEAD_DIM)
    angles = positions.astype(jnp.float32)[None, :] * freqs[:, None]
    return jnp.cos(angles), jnp.sin(angles)


def pair_lists(end_rows, blocks):
    at = jnp.arange(blocks, dtype=jnp.int32) * BLOCK
    after = end_rows[:, None, :] + 1
    first = jnp.max(jnp.where(after <= at[None, :, None], after, 0), -1) // BLOCK
    codes = [(i, i - d) for d in range(1, blocks) for i in range(d, blocks)]
    query = jnp.array([i for i, _ in codes], jnp.int32)
    key = jnp.array([j for _, j in codes], jnp.int32)
    lowest = jnp.stack([first[:, i] for i, _ in codes], 1)
    valid = key[None] >= lowest
    place = jnp.cumsum(valid.astype(jnp.int32), 1) - 1
    slot = jnp.arange(len(codes), dtype=jnp.int32)
    chosen = valid[:, :, None] & (place[:, :, None] == slot)
    listed = jnp.sum(jnp.where(chosen, (query * blocks + key)[None, :, None], 0), 1)
    counts = jnp.sum(valid.astype(jnp.int32), 1)
    listed = jnp.where(slot[None] < counts[:, None], listed, blocks - 1)
    return listed, jnp.max(counts).reshape(1)


def block_of(ref, part, slab, b, rows):
    per = BLOCK // rows
    return jnp.concatenate(
        [
            ref[
                b * per + r,
                part * HEAD_DIM : (part + 1) * HEAD_DIM,
                slab * rows : (slab + 1) * rows,
            ]
            for r in range(per)
        ],
        axis=1,
    )


def mask_of(starts, i, j):
    place = lax.broadcasted_iota(jnp.int32, (1, BLOCK), 1) + i * BLOCK
    key = lax.broadcasted_iota(jnp.int32, (BLOCK, BLOCK), 0) + j * BLOCK
    return (key >= starts) & (key <= place)


def starts_of(ends_ref, slab, b):
    place = lax.broadcasted_iota(jnp.int32, (1, BLOCK), 1) + b * BLOCK
    start = jnp.zeros((1, BLOCK), jnp.int32)
    for d in range(ends_ref.shape[1] - 1):
        after = ends_ref[slab, d] + 1
        start = jnp.where(place >= after, after, start)
    return start


def forward_kernel(
    ends_ref, pairs_ref, count_ref, in_ref, out_ref, stats_ref, q_s, k_s, vt_s, start_s, top_s, sum_s, acc_s
):
    slabs = ends_ref.shape[0]
    n_src = in_ref.shape[0]
    rows = in_ref.shape[2] // slabs
    per = BLOCK // rows
    blocks = n_src // per
    f32, bf16 = jnp.float32, jnp.bfloat16

    for s in range(slabs):
        for b in range(blocks):
            at = s * blocks + b
            q_s[at] = block_of(in_ref, 0, s, b, rows)
            k_s[at] = block_of(in_ref, 1, s, b, rows).T
            vt_s[at] = block_of(in_ref, 2, s, b, rows)
            start_s[at] = starts_of(ends_ref, s, b)

    def scores(s, i, j):
        raw = jnp.dot(k_s[s * blocks + j], q_s[s * blocks + i], preferred_element_type=f32)
        return jnp.where(mask_of(start_s[s * blocks + i], i, j), raw, -jnp.inf)

    def weighted(w, at):
        over_keys = (((0,), (1,)), ((), ()))
        return lax.dot_general(
            w.astype(bf16), vt_s[at], over_keys, preferred_element_type=f32
        ).T

    def diagonal(i, _):
        done = []
        for s in range(slabs):
            raw = scores(s, i, i)
            top = jnp.max(raw, axis=0, keepdims=True)
            w = jnp.exp(raw - top)
            total = jnp.sum(w, axis=0, keepdims=True)
            acc = weighted(w, s * blocks + i)
            done.append((top, total, acc))
        for s in range(slabs):
            at = s * blocks + i
            top_s[at], sum_s[at], acc_s[at] = done[s]
        return 0

    lax.fori_loop(0, blocks, diagonal, 0, unroll=True)

    def below(step, _):
        done = []
        for s in range(slabs):
            code = pairs_ref[s, step]
            i, j = lax.div(code, blocks), lax.rem(code, blocks)
            at = s * blocks + i
            raw = scores(s, i, j)
            old = top_s[at]
            top = jnp.maximum(old, jnp.max(raw, axis=0, keepdims=True))
            fade = jnp.exp(old - top)
            w = jnp.exp(raw - top)
            total = sum_s[at] * fade + jnp.sum(w, axis=0, keepdims=True)
            acc = acc_s[at] * fade + weighted(w, s * blocks + j)
            done.append((at, top, total, acc))
        for at, top, total, acc in done:
            top_s[at], sum_s[at], acc_s[at] = top, total, acc
        return 0

    lax.fori_loop(0, count_ref[0], below, 0)

    for s in range(slabs):
        for b in range(blocks):
            at = s * blocks + b
            inv = 1.0 / sum_s[at]
            stats_ref[at, 0:1, :] = top_s[at]
            stats_ref[at, 1:2, :] = inv
            ctx = (acc_s[at] * inv).astype(bf16)
            for r in range(per):
                out_ref[b * per + r, :, s * rows : (s + 1) * rows] = ctx[
                    :, r * rows : (r + 1) * rows
                ]


def backward_kernel(
    ends_ref,
    pairs_ref,
    count_ref,
    in_ref,
    grad_ref,
    ctx_ref,
    stats_ref,
    cos_ref,
    sin_ref,
    out_ref,
    q_s,
    kt_s,
    k_s,
    v_s,
    g_s,
    start_s,
    delta_s,
    dq_s,
    dk_s,
    dv_s,
):
    slabs = ends_ref.shape[0]
    n_src = in_ref.shape[0]
    rows = in_ref.shape[2] // slabs
    per = BLOCK // rows
    blocks = n_src // per
    f32, bf16 = jnp.float32, jnp.bfloat16
    hd = HEAD_DIM

    for s in range(slabs):
        for b in range(blocks):
            at = s * blocks + b
            kt = block_of(in_ref, 1, s, b, rows)
            grad = block_of(grad_ref, 0, s, b, rows)
            ctx = block_of(ctx_ref, 0, s, b, rows)
            q_s[at] = block_of(in_ref, 0, s, b, rows)
            kt_s[at] = kt
            k_s[at] = kt.T
            v_s[at] = block_of(in_ref, 2, s, b, rows).T
            g_s[at] = grad
            start_s[at] = starts_of(ends_ref, s, b)
            delta_s[at] = jnp.sum(grad.astype(f32) * ctx.astype(f32), axis=0, keepdims=True)

    trans = (((1,), (1,)), ((), ()))

    def terms(s, i, j):
        qi, kj = s * blocks + i, s * blocks + j
        query, grad = q_s[qi], g_s[qi]
        raw = jnp.dot(k_s[kj], query, preferred_element_type=f32)
        raw = jnp.where(mask_of(start_s[qi], i, j), raw, -jnp.inf)
        probs = jnp.exp(raw - stats_ref[qi, 0:1, :]) * stats_ref[qi, 1:2, :]
        dp = jnp.dot(v_s[kj], grad, preferred_element_type=f32)
        ds = (probs * (dp - delta_s[qi])).astype(bf16)
        dv = lax.dot_general(grad, probs.astype(bf16), trans, preferred_element_type=f32)
        dk = lax.dot_general(query, ds, trans, preferred_element_type=f32)
        dq = jnp.dot(kt_s[kj], ds, preferred_element_type=f32)
        return qi, kj, dq, dk, dv

    def diagonal(i, _):
        done = [terms(s, i, i) for s in range(slabs)]
        for qi, kj, dq, dk, dv in done:
            dq_s[qi], dk_s[kj], dv_s[kj] = dq, dk, dv
        return 0

    lax.fori_loop(0, blocks, diagonal, 0, unroll=True)

    def below(step, _):
        done = []
        for s in range(slabs):
            code = pairs_ref[s, step]
            qi, kj, dq, dk, dv = terms(s, lax.div(code, blocks), lax.rem(code, blocks))
            done.append((qi, kj, dq_s[qi] + dq, dk_s[kj] + dk, dv_s[kj] + dv))
        for qi, kj, dq, dk, dv in done:
            dq_s[qi], dk_s[kj], dv_s[kj] = dq, dk, dv
        return 0

    lax.fori_loop(0, count_ref[0], below, 0)

    for s in range(slabs):
        for b in range(blocks):
            at = s * blocks + b
            for r in range(per):
                lanes = slice(r * rows, (r + 1) * rows)
                src, here = b * per + r, slice(s * rows, (s + 1) * rows)
                cosine, sine = cos_ref[src], sin_ref[src]
                for n, grads, factor in ((0, dq_s, hd**-0.5), (1, dk_s, None)):
                    x, y = grads[at, :HALF, lanes], grads[at, HALF:, lanes]
                    if factor is not None:
                        x, y = x * factor, y * factor
                    out_ref[src, n * hd : n * hd + HALF, here] = (
                        x * cosine + y * sine
                    ).astype(bf16)
                    out_ref[src, n * hd + HALF : (n + 1) * hd, here] = (
                        y * cosine - x * sine
                    ).astype(bf16)
                out_ref[src, 2 * hd : 3 * hd, here] = dv_s[at, :, lanes].astype(bf16)


SMEM = pl.BlockSpec(memory_space=pltpu.SMEM)
VMEM = pl.BlockSpec(memory_space=pltpu.VMEM)
VMEM_LIMIT = 48 * 1024 * 1024


def attend(received, ends, pairs, count):
    n_src, _, tok = received.shape
    n = n_src * tok // BLOCK
    bf16, f32 = jnp.bfloat16, jnp.float32
    wide = pltpu.VMEM((n, HEAD_DIM, BLOCK), bf16)
    row = pltpu.VMEM((n, 1, BLOCK), f32)
    return pl.pallas_call(
        forward_kernel,
        out_shape=(
            jax.ShapeDtypeStruct((n_src, HEAD_DIM, tok), bf16),
            jax.ShapeDtypeStruct((n, 2, BLOCK), f32),
        ),
        in_specs=[SMEM, SMEM, SMEM, VMEM],
        out_specs=(VMEM, VMEM),
        scratch_shapes=[
            wide,
            pltpu.VMEM((n, BLOCK, HEAD_DIM), bf16),
            wide,
            pltpu.VMEM((n, 1, BLOCK), jnp.int32),
            row,
            row,
            pltpu.VMEM((n, HEAD_DIM, BLOCK), f32),
        ],
        compiler_params=pltpu.CompilerParams(vmem_limit_bytes=VMEM_LIMIT),
        cost_estimate=pl.CostEstimate(
            flops=8 * 10**9, bytes_accessed=4 * 2**20, transcendentals=3 * 2**20
        ),
        name="attend",
    )(ends, pairs, count, received)


def attend_back(received, grads, context, stats, ends, pairs, count, cos_all, sin_all):
    n_src, _, tok = received.shape
    n = n_src * tok // BLOCK
    bf16, f32 = jnp.bfloat16, jnp.float32
    wide = pltpu.VMEM((n, HEAD_DIM, BLOCK), bf16)
    tall = pltpu.VMEM((n, BLOCK, HEAD_DIM), bf16)
    total = pltpu.VMEM((n, HEAD_DIM, BLOCK), f32)
    return pl.pallas_call(
        backward_kernel,
        out_shape=jax.ShapeDtypeStruct(received.shape, bf16),
        in_specs=[SMEM, SMEM, SMEM] + [VMEM] * 6,
        out_specs=VMEM,
        scratch_shapes=[
            wide,
            wide,
            tall,
            tall,
            wide,
            pltpu.VMEM((n, 1, BLOCK), jnp.int32),
            pltpu.VMEM((n, 1, BLOCK), f32),
            total,
            total,
            total,
        ],
        compiler_params=pltpu.CompilerParams(vmem_limit_bytes=VMEM_LIMIT),
        cost_estimate=pl.CostEstimate(
            flops=16 * 10**9, bytes_accessed=8 * 2**20, transcendentals=3 * 2**20
        ),
        name="attend_back",
    )(ends, pairs, count, received, grads, context, stats, cos_all, sin_all)


def on_device(
    tokens,
    segment_ids,
    end_rows,
    input_norm_gain,
    query_weight,
    key_weight,
    value_weight,
    out_weight,
    head_weight,
    branch_grad,
):
    del segment_ids
    bf16, f32 = jnp.bfloat16, jnp.float32
    n_ctx, n_x, n_core = (lax.axis_size(a) for a in ("ctx", "x", "core"))
    rank = lax.axis_index("ctx")
    core = lax.axis_index("core")
    slabs, rows, model = tokens.shape
    docs = end_rows.shape[1]
    tok = slabs * rows
    width = HEADS * HEAD_DIM
    kv_width = KV_HEADS * HEAD_DIM
    qkv = width + 2 * kv_width
    swap = [(c, n_core - 1 - c) for c in range(n_core)]

    weights = lax.all_gather(
        jnp.concatenate([query_weight, key_weight, value_weight, out_weight], 1),
        ("ctx", "x", "core"),
        axis=0,
        tiled=True,
    )

    flat = tokens.reshape(tok, model)
    grad_out = branch_grad.reshape(tok, model)
    wide = flat.astype(f32)
    inverse_norm = lax.rsqrt(jnp.mean(wide * wide, -1, keepdims=True) + eps)
    normed = (wide * inverse_norm * input_norm_gain).astype(bf16)

    def by_core(values):
        split = values.T.reshape(model // (16 * n_core), n_core, 16, tok)
        mine = lax.dynamic_index_in_dim(split, core, 1, keepdims=False).reshape(-1, tok)
        other = lax.dynamic_index_in_dim(split, 1 - core, 1, keepdims=False).reshape(-1, tok)
        return mine, lax.ppermute(other, "core", swap)

    normed_mine, normed_other = by_core(normed)
    grad_out_mine, grad_out_other = by_core(grad_out)

    first = rank * rows
    cos_all, sin_all = rotation_tables(jnp.arange(n_ctx * rows, dtype=jnp.int32))
    cos_here, sin_here = rotation_tables(first + jnp.arange(rows, dtype=jnp.int32))
    cos_here = jnp.tile(cos_here, (1, slabs))[None]
    sin_here = jnp.tile(sin_here, (1, slabs))[None]
    over = (((0,), (1,)), ((), ()))
    projected = lax.dot_general(weights[:, :qkv], normed, over, preferred_element_type=f32)
    turning = projected[: width + kv_width].reshape(HEADS + KV_HEADS, 2, HALF, tok)
    front, back = turning[:, 0], turning[:, 1]
    turned = jnp.concatenate(
        [front * cos_here - back * sin_here, back * cos_here + front * sin_here], 1
    )
    query = (turned[:HEADS] * (HEAD_DIM**-0.5)).astype(bf16)
    keys = jnp.repeat(turned[HEADS:].astype(bf16), GROUP, axis=0)
    values = projected[width + kv_width :].astype(bf16).reshape(KV_HEADS, HEAD_DIM, tok)
    values = jnp.repeat(values, GROUP, axis=0)
    send = jnp.concatenate([query, keys, values], 1)
    received = lax.all_to_all(send, "ctx", split_axis=0, concat_axis=0, tiled=True)
    context_grad = lax.dot_general(
        weights[:, qkv:], grad_out, over, preferred_element_type=f32
    ).astype(bf16)
    grads_in = lax.all_to_all(
        context_grad.reshape(HEADS, HEAD_DIM, tok), "ctx", split_axis=0, concat_axis=0, tiled=True
    )

    pairs, count = pair_lists(end_rows, n_ctx * rows // BLOCK)
    context_head, stats = attend(received, end_rows, pairs, count)
    context_head, grads_in = lax.optimization_barrier((context_head, grads_in))
    context = lax.all_to_all(context_head, "ctx", split_axis=0, concat_axis=0, tiled=True)

    def by_source(table):
        return jnp.swapaxes(table.reshape(HALF, n_ctx, rows), 0, 1)

    results = attend_back(
        received,
        grads_in,
        context_head,
        stats,
        end_rows,
        pairs,
        count,
        by_source(cos_all),
        by_source(sin_all),
    )
    back_home = lax.all_to_all(results, "ctx", split_axis=0, concat_axis=0, tiled=True)
    last = (((1,), (1,)), ((), ()))

    def both_cores(a, b, c, d):
        return lax.dot_general(
            jnp.concatenate([a, c], 1),
            jnp.concatenate([b, d], 1),
            last,
            preferred_element_type=f32,
        ).astype(bf16)

    context = context.reshape(width, tok)
    context_other = lax.ppermute(context, "core", swap)
    partial_out = both_cores(grad_out_mine, context, grad_out_other, context_other)

    branch = lax.dot_general(context, weights[:, qkv:], over, preferred_element_type=f32)
    branch = branch.astype(bf16)
    here = jnp.arange(slabs, dtype=jnp.int32)
    marks = (
        (end_rows[:, :, None, None] == first + jnp.arange(rows, dtype=jnp.int32))
        & (here[:, None, None, None] == here[:, None])
    ).astype(bf16)
    marks = marks.reshape(slabs * docs, tok)
    picked = jnp.dot(marks, flat, preferred_element_type=f32) + jnp.dot(
        marks, branch, preferred_element_type=f32
    )
    picked = picked * lax.rsqrt(jnp.mean(picked * picked, -1, keepdims=True) + eps)
    rewards = jnp.sum(picked * head_weight, -1).reshape(slabs, docs)
    hd = HEAD_DIM
    back_home, partial_out = lax.optimization_barrier((back_home, partial_out))
    pieces_out = lax.all_to_all(
        partial_out, ("ctx", "x"), split_axis=0, concat_axis=0, tiled=True
    )
    dquery = back_home[:, :hd].reshape(width, tok)

    def over_group(heads):
        heads = heads.astype(f32).reshape(KV_HEADS, GROUP, hd, tok)
        return jnp.sum(heads, 1).astype(bf16).reshape(kv_width, tok)

    dkey = over_group(back_home[:, hd : 2 * hd])
    dvalue = over_group(back_home[:, 2 * hd :])
    grads = jnp.concatenate([dquery, dkey, dvalue], 0)
    grads_other = lax.ppermute(grads, "core", swap)
    partial = both_cores(normed_mine, grads, normed_other, grads_other)
    partial, grads, context = lax.optimization_barrier((partial, grads, context))
    chunks, parts = n_ctx * n_x, []
    rest = rewards.reshape(-1)
    for _ in range(3):
        part = lax.reduce_precision(rest, 8, 7)
        parts.append(part)
        rest = rest - part
    riders = jnp.stack(parts, 0).astype(bf16)
    extra = 128
    riders = jnp.pad(riders, ((0, 16 - len(parts)), (0, extra - riders.shape[1])))
    partial = jnp.concatenate([partial, jnp.tile(riders, (chunks, 1))], 1)
    pieces = lax.all_to_all(partial, ("ctx", "x"), split_axis=0, concat_axis=0, tiled=True)
    dnormed = lax.dot_general(grads, weights[:, :qkv], over, preferred_element_type=f32)
    scaled = dnormed * input_norm_gain
    centered = wide * inverse_norm
    grad_tokens = inverse_norm * (
        scaled - centered * jnp.mean(scaled * centered, -1, keepdims=True)
    )
    pieces = pieces.reshape(chunks, -1, qkv + extra)
    summed = jnp.sum(pieces[:, :, :qkv].astype(f32), 0)
    summed_out = jnp.sum(pieces_out.reshape(chunks, -1, width).astype(f32), 0)
    riders = pieces[:, : len(parts), qkv:].reshape(n_ctx, n_x, len(parts), extra)
    riders = lax.dynamic_index_in_dim(riders, lax.axis_index("x"), 1, keepdims=False)
    rewards = jnp.sum(riders[:, :, : slabs * docs].astype(f32), (0, 1)).reshape(slabs, docs)
    return (
        branch.reshape(tokens.shape),
        rewards,
        grad_tokens.astype(bf16).reshape(tokens.shape),
        summed[:, :width],
        summed[:, width : width + kv_width],
        summed[:, width + kv_width :],
        summed_out,
    )


def solution(mesh):
    n_ctx, n_fsdp = mesh.devices.shape
    chips = Mesh(mesh.devices.reshape(n_ctx, n_fsdp // 2, 2), ("ctx", "x", "core"))
    fsdp = ("x", "core")
    rows = P(("ctx", "x", "core"), None)
    acts = P(fsdp, "ctx", None)
    return jax.shard_map(
        on_device,
        mesh=chips,
        in_specs=(
            acts,
            P(fsdp, None),
            P(fsdp, None),
            P(),
            rows,
            rows,
            rows,
            rows,
            P(),
            acts,
        ),
        out_specs=(acts, P(fsdp, None), acts, rows, rows, rows, rows),
        check_vma=False,
    )
```

```python
import jax
import jax.numpy as jnp
from jax import lax
from jax.experimental import pallas as pl
from jax.experimental.pallas import tpu as pltpu
from jax.sharding import Mesh
from jax.sharding import PartitionSpec as P

HEADS = 16
KV_HEADS = 4
HEAD_DIM = 64
GROUP = HEADS // KV_HEADS
SLABS_HERE = 3
SET_OF = (0, 0, 1)
UNITS, SETS = 3, 2
HALF = HEAD_DIM // 2
BLOCK = 256

eps = 1e-05
base_theta = 500000.0


def rotation_tables(positions):
    freqs = base_theta ** (-(2.0 * jnp.arange(HALF, dtype=jnp.float32)) / HEAD_DIM)
    angles = positions.astype(jnp.float32)[None, :] * freqs[:, None]
    return jnp.cos(angles), jnp.sin(angles)


def pair_lists(end_rows, blocks):
    at = jnp.arange(blocks, dtype=jnp.int32) * BLOCK
    after = end_rows[:, None, :] + 1
    first = jnp.max(jnp.where(after <= at[None, :, None], after, 0), -1) // BLOCK
    codes = [(i, i - d) for d in range(1, blocks) for i in range(d, blocks)]
    query = jnp.array([i for i, _ in codes], jnp.int32)
    key = jnp.array([j for _, j in codes], jnp.int32)
    lowest = jnp.stack([first[:, i] for i, _ in codes], 1)
    valid = key[None] >= lowest
    place = jnp.cumsum(valid.astype(jnp.int32), 1) - 1
    slot = jnp.arange(len(codes), dtype=jnp.int32)
    chosen = valid[:, :, None] & (place[:, :, None] == slot)
    listed = jnp.sum(jnp.where(chosen, (query * blocks + key)[None, :, None], 0), 1)
    counts = jnp.sum(valid.astype(jnp.int32), 1)
    listed = jnp.where(slot[None] < counts[:, None], listed, blocks - 1)
    return listed, jnp.max(counts).reshape(1)


def block_of(ref, part, b):
    per = BLOCK // ref.shape[2]
    at = slice(part * HEAD_DIM, (part + 1) * HEAD_DIM)
    return jnp.concatenate([ref[b * per + r, at, :] for r in range(per)], axis=1)


def mask_of(starts, i, j):
    place = lax.broadcasted_iota(jnp.int32, (1, BLOCK), 1) + i * BLOCK
    key = lax.broadcasted_iota(jnp.int32, (BLOCK, BLOCK), 0) + j * BLOCK
    return (key >= starts) & (key <= place)


def starts_of(ends_ref, slab, b):
    place = lax.broadcasted_iota(jnp.int32, (1, BLOCK), 1) + b * BLOCK
    start = jnp.zeros((1, BLOCK), jnp.int32)
    for d in range(ends_ref.shape[1] - 1):
        after = ends_ref[slab, d] + 1
        start = jnp.where(place >= after, after, start)
    return start


def forward_kernel(
    ends_ref, pairs_ref, count_ref, in_ref, out_ref, stats_ref, q_s, k_s, vt_s, start_s, top_s, sum_s, acc_s
):
    n_src, _, rows = in_ref.shape
    per = BLOCK // rows
    blocks = n_src // per
    f32, bf16 = jnp.float32, jnp.bfloat16

    for b in range(blocks):
        for u in range(UNITS):
            q_s[u * blocks + b] = block_of(in_ref, u, b)
        for t in range(SETS):
            at = t * blocks + b
            k_s[at] = block_of(in_ref, UNITS + t, b).T
            vt_s[at] = block_of(in_ref, UNITS + SETS + t, b)
            start_s[at] = starts_of(ends_ref, t, b)

    def scores(u, i, j, mask):
        keys = k_s[SET_OF[u] * blocks + j]
        raw = jnp.dot(keys, q_s[u * blocks + i], preferred_element_type=f32)
        return jnp.where(mask, raw, -jnp.inf)

    def weighted(w, at):
        over_keys = (((0,), (1,)), ((), ()))
        return lax.dot_general(
            w.astype(bf16), vt_s[at], over_keys, preferred_element_type=f32
        ).T

    def diagonal(i, _):
        masks = [mask_of(start_s[t * blocks + i], i, i) for t in range(SETS)]
        done = []
        for u in range(UNITS):
            t = SET_OF[u]
            raw = scores(u, i, i, masks[t])
            top = jnp.max(raw, axis=0, keepdims=True)
            w = jnp.exp(raw - top)
            total = jnp.sum(w, axis=0, keepdims=True)
            done.append((u * blocks + i, top, total, weighted(w, t * blocks + i)))
        for at, top, total, acc in done:
            top_s[at], sum_s[at], acc_s[at] = top, total, acc
        return 0

    lax.fori_loop(0, blocks, diagonal, 0, unroll=True)

    def below(step, _):
        codes = [pairs_ref[t, step] for t in range(SETS)]
        places = [(lax.div(code, blocks), lax.rem(code, blocks)) for code in codes]
        masks = [mask_of(start_s[t * blocks + i], i, j) for t, (i, j) in enumerate(places)]
        done = []
        for u in range(UNITS):
            t = SET_OF[u]
            i, j = places[t]
            at = u * blocks + i
            raw = scores(u, i, j, masks[t])
            old = top_s[at]
            top = jnp.maximum(old, jnp.max(raw, axis=0, keepdims=True))
            fade = jnp.exp(old - top)
            w = jnp.exp(raw - top)
            total = sum_s[at] * fade + jnp.sum(w, axis=0, keepdims=True)
            acc = acc_s[at] * fade + weighted(w, t * blocks + j)
            done.append((at, top, total, acc))
        for at, top, total, acc in done:
            top_s[at], sum_s[at], acc_s[at] = top, total, acc
        return 0

    lax.fori_loop(0, count_ref[0], below, 0)

    for u in range(UNITS):
        for b in range(blocks):
            at = u * blocks + b
            inv = 1.0 / sum_s[at]
            stats_ref[at, 0:1, :] = top_s[at]
            stats_ref[at, 1:2, :] = inv
            ctx = (acc_s[at] * inv).astype(bf16)
            for r in range(per):
                out_ref[b * per + r, u * HEAD_DIM : (u + 1) * HEAD_DIM, :] = ctx[
                    :, r * rows : (r + 1) * rows
                ]


def backward_kernel(
    ends_ref,
    pairs_ref,
    count_ref,
    in_ref,
    grad_ref,
    ctx_ref,
    stats_ref,
    cos_ref,
    sin_ref,
    out_ref,
    q_s,
    kt_s,
    k_s,
    v_s,
    g_s,
    start_s,
    delta_s,
    dq_s,
    dk_s,
    dv_s,
):
    n_src, _, rows = in_ref.shape
    per = BLOCK // rows
    blocks = n_src // per
    f32, bf16 = jnp.float32, jnp.bfloat16
    hd = HEAD_DIM

    for b in range(blocks):
        for u in range(UNITS):
            at = u * blocks + b
            grad = block_of(grad_ref, u, b)
            ctx = block_of(ctx_ref, u, b)
            q_s[at] = block_of(in_ref, u, b)
            g_s[at] = grad
            delta_s[at] = jnp.sum(grad.astype(f32) * ctx.astype(f32), axis=0, keepdims=True)
        for t in range(SETS):
            at = t * blocks + b
            kt = block_of(in_ref, UNITS + t, b)
            kt_s[at] = kt
            k_s[at] = kt.T
            v_s[at] = block_of(in_ref, UNITS + SETS + t, b).T
            start_s[at] = starts_of(ends_ref, t, b)

    trans = (((1,), (1,)), ((), ()))

    def terms(places):
        masks = [mask_of(start_s[t * blocks + i], i, j) for t, (i, j) in enumerate(places)]
        dqs, dks, dvs = [], [None] * SETS, [None] * SETS
        for u in range(UNITS):
            t = SET_OF[u]
            i, j = places[t]
            qi, kj = u * blocks + i, t * blocks + j
            query, grad = q_s[qi], g_s[qi]
            raw = jnp.dot(k_s[kj], query, preferred_element_type=f32)
            raw = jnp.where(masks[t], raw, -jnp.inf)
            probs = jnp.exp(raw - stats_ref[qi, 0:1, :]) * stats_ref[qi, 1:2, :]
            dp = jnp.dot(v_s[kj], grad, preferred_element_type=f32)
            ds = (probs * (dp - delta_s[qi])).astype(bf16)
            dv = lax.dot_general(grad, probs.astype(bf16), trans, preferred_element_type=f32)
            dk = lax.dot_general(query, ds, trans, preferred_element_type=f32)
            dqs.append((qi, jnp.dot(kt_s[kj], ds, preferred_element_type=f32)))
            dks[t] = (kj, dk if dks[t] is None else dks[t][1] + dk)
            dvs[t] = (kj, dv if dvs[t] is None else dvs[t][1] + dv)
        return ((dq_s, dqs), (dk_s, dks), (dv_s, dvs))

    def diagonal(i, _):
        for ref, values in terms([(i, i)] * SETS):
            for at, value in values:
                ref[at] = value
        return 0

    lax.fori_loop(0, blocks, diagonal, 0, unroll=True)

    def below(step, _):
        codes = [pairs_ref[t, step] for t in range(SETS)]
        places = [(lax.div(code, blocks), lax.rem(code, blocks)) for code in codes]
        done = [
            (ref, at, ref[at] + value) for ref, values in terms(places) for at, value in values
        ]
        for ref, at, value in done:
            ref[at] = value
        return 0

    lax.fori_loop(0, count_ref[0], below, 0)

    def turned_back(grads, at, lanes, src, factor):
        x, y = grads[at, :HALF, lanes] * factor, grads[at, HALF:, lanes] * factor
        cosine, sine = cos_ref[src], sin_ref[src]
        return (x * cosine + y * sine).astype(bf16), (y * cosine - x * sine).astype(bf16)

    for b in range(blocks):
        for r in range(per):
            lanes, src = slice(r * rows, (r + 1) * rows), b * per + r
            for u in range(UNITS):
                x, y = turned_back(dq_s, u * blocks + b, lanes, src, hd**-0.5)
                out_ref[src, u * hd : u * hd + HALF, :] = x
                out_ref[src, u * hd + HALF : (u + 1) * hd, :] = y
            for t in range(SETS):
                at, to = t * blocks + b, UNITS + t
                x, y = turned_back(dk_s, at, lanes, src, 1.0)
                out_ref[src, to * hd : to * hd + HALF, :] = x
                out_ref[src, to * hd + HALF : (to + 1) * hd, :] = y
                to += SETS
                out_ref[src, to * hd : (to + 1) * hd, :] = dv_s[at, :, lanes].astype(bf16)


SMEM = pl.BlockSpec(memory_space=pltpu.SMEM)
VMEM = pl.BlockSpec(memory_space=pltpu.VMEM)
VMEM_LIMIT = 48 * 1024 * 1024


def attend(received, ends, pairs, count):
    n_src, _, rows = received.shape
    blocks = n_src * rows // BLOCK
    n, m = UNITS * blocks, SETS * blocks
    bf16, f32 = jnp.bfloat16, jnp.float32
    row = pltpu.VMEM((n, 1, BLOCK), f32)
    return pl.pallas_call(
        forward_kernel,
        out_shape=(
            jax.ShapeDtypeStruct((n_src, UNITS * HEAD_DIM, rows), bf16),
            jax.ShapeDtypeStruct((n, 2, BLOCK), f32),
        ),
        in_specs=[SMEM, SMEM, SMEM, VMEM],
        out_specs=(VMEM, VMEM),
        scratch_shapes=[
            pltpu.VMEM((n, HEAD_DIM, BLOCK), bf16),
            pltpu.VMEM((m, BLOCK, HEAD_DIM), bf16),
            pltpu.VMEM((m, HEAD_DIM, BLOCK), bf16),
            pltpu.VMEM((m, 1, BLOCK), jnp.int32),
            row,
            row,
            pltpu.VMEM((n, HEAD_DIM, BLOCK), f32),
        ],
        compiler_params=pltpu.CompilerParams(vmem_limit_bytes=VMEM_LIMIT),
        cost_estimate=pl.CostEstimate(
            flops=8 * 10**9, bytes_accessed=4 * 2**20, transcendentals=3 * 2**20
        ),
        name="attend",
    )(ends, pairs, count, received)


def attend_back(received, grads, context, stats, ends, pairs, count, cos_all, sin_all):
    n_src, _, rows = received.shape
    blocks = n_src * rows // BLOCK
    n, m = UNITS * blocks, SETS * blocks
    bf16, f32 = jnp.bfloat16, jnp.float32
    tall = pltpu.VMEM((m, BLOCK, HEAD_DIM), bf16)
    return pl.pallas_call(
        backward_kernel,
        out_shape=jax.ShapeDtypeStruct(received.shape, bf16),
        in_specs=[SMEM, SMEM, SMEM] + [VMEM] * 6,
        out_specs=VMEM,
        scratch_shapes=[
            pltpu.VMEM((n, HEAD_DIM, BLOCK), bf16),
            pltpu.VMEM((m, HEAD_DIM, BLOCK), bf16),
            tall,
            tall,
            pltpu.VMEM((n, HEAD_DIM, BLOCK), bf16),
            pltpu.VMEM((m, 1, BLOCK), jnp.int32),
            pltpu.VMEM((n, 1, BLOCK), f32),
            pltpu.VMEM((n, HEAD_DIM, BLOCK), f32),
            pltpu.VMEM((m, HEAD_DIM, BLOCK), f32),
            pltpu.VMEM((m, HEAD_DIM, BLOCK), f32),
        ],
        compiler_params=pltpu.CompilerParams(vmem_limit_bytes=VMEM_LIMIT),
        cost_estimate=pl.CostEstimate(
            flops=16 * 10**9, bytes_accessed=8 * 2**20, transcendentals=3 * 2**20
        ),
        name="attend_back",
    )(ends, pairs, count, received, grads, context, stats, cos_all, sin_all)


def to_units(heads):
    pairs = heads.reshape(HEADS // 2, 2, HEAD_DIM, -1)
    first, second, last = jnp.split(pairs, SLABS_HERE, axis=-1)
    return jnp.stack(
        [
            jnp.concatenate([own[:, 0], own[:, 1], last[:, e]], 1)
            for e, own in enumerate((first, second))
        ],
        1,
    )


def to_sets(heads):
    first, second, last = jnp.split(heads, SLABS_HERE, axis=-1)
    both = jnp.stack([jnp.concatenate([own, last], 1) for own in (first, second)], 1)
    return jnp.repeat(both, GROUP // 2, axis=0)


def from_units(units):
    rows = units.shape[-1]
    units = units.reshape(HEADS // 2, 2, UNITS, HEAD_DIM, rows)
    parts = [units[:, 0, :2], units[:, 1, :2], units[:, :, 2]]
    return jnp.concatenate(parts, -1).reshape(HEADS * HEAD_DIM, -1)


def from_sets(sets):
    rows = sets.shape[-1]
    sets = sets.astype(jnp.float32)
    sets = sets.reshape(KV_HEADS, GROUP // 2, 2, SETS, HEAD_DIM, rows)
    parts = [
        jnp.sum(sets[:, :, 0, 0], 1),
        jnp.sum(sets[:, :, 1, 0], 1),
        jnp.sum(sets[:, :, :, 1], (1, 2)),
    ]
    return jnp.concatenate(parts, -1).astype(jnp.bfloat16).reshape(KV_HEADS * HEAD_DIM, -1)


def on_device(
    tokens,
    segment_ids,
    end_rows,
    input_norm_gain,
    query_weight,
    key_weight,
    value_weight,
    out_weight,
    head_weight,
    branch_grad,
):
    del segment_ids
    bf16, f32 = jnp.bfloat16, jnp.float32
    n_ctx, n_x, n_core = (lax.axis_size(a) for a in ("ctx", "x", "core"))
    rank = lax.axis_index("ctx")
    core = lax.axis_index("core")
    slabs, rows, model = tokens.shape
    docs = end_rows.shape[1]
    tok = slabs * rows
    width = HEADS * HEAD_DIM
    kv_width = KV_HEADS * HEAD_DIM
    qkv = width + 2 * kv_width
    swap = [(c, n_core - 1 - c) for c in range(n_core)]

    weights = lax.all_gather(
        jnp.concatenate([query_weight, key_weight, value_weight, out_weight], 1),
        ("ctx", "x", "core"),
        axis=0,
        tiled=True,
    )

    flat = tokens.reshape(tok, model)
    grad_out = branch_grad.reshape(tok, model)
    wide = flat.astype(f32)
    inverse_norm = lax.rsqrt(jnp.mean(wide * wide, -1, keepdims=True) + eps)
    normed = (wide * inverse_norm * input_norm_gain).astype(bf16)

    split = grad_out.T.reshape(model // (16 * n_core), n_core, 16, tok)
    mine = lax.dynamic_index_in_dim(split, core, 1, keepdims=False).reshape(-1, tok)
    other = lax.dynamic_index_in_dim(split, 1 - core, 1, keepdims=False).reshape(-1, tok)
    grad_out_both = jnp.concatenate([mine, lax.ppermute(other, "core", swap)], 1)
    n_fsdp = n_x * n_core
    normed_rows = jnp.swapaxes(normed.T.reshape(n_ctx, n_fsdp, 16, tok), 0, 1)
    normed_rows = normed_rows.reshape(model, tok)

    first = rank * rows
    cos_all, sin_all = rotation_tables(jnp.arange(n_ctx * rows, dtype=jnp.int32))
    cos_here, sin_here = rotation_tables(first + jnp.arange(rows, dtype=jnp.int32))
    cos_here = jnp.tile(cos_here, (1, slabs))[None]
    sin_here = jnp.tile(sin_here, (1, slabs))[None]
    over = (((0,), (1,)), ((), ()))
    projected = lax.dot_general(weights[:, :qkv], normed, over, preferred_element_type=f32)
    turning = projected[: width + kv_width].reshape(HEADS + KV_HEADS, 2, HALF, tok)
    front, back = turning[:, 0], turning[:, 1]
    turned = jnp.concatenate(
        [front * cos_here - back * sin_here, back * cos_here + front * sin_here], 1
    )
    query = (turned[:HEADS] * (HEAD_DIM**-0.5)).astype(bf16)
    keys = turned[HEADS:].astype(bf16)
    values = projected[width + kv_width :].astype(bf16).reshape(KV_HEADS, HEAD_DIM, tok)
    send = jnp.concatenate([to_units(query), to_sets(keys), to_sets(values)], 2)
    send = send.reshape(HEADS, -1, rows)
    received = lax.all_to_all(send, "ctx", split_axis=0, concat_axis=0, tiled=True)
    context_grad = lax.dot_general(
        weights[:, qkv:], grad_out, over, preferred_element_type=f32
    ).astype(bf16)
    grads_in = lax.all_to_all(
        to_units(context_grad).reshape(HEADS, -1, rows), "ctx", split_axis=0, concat_axis=0, tiled=True
    )

    own = lax.dynamic_index_in_dim(end_rows, lax.rem(rank, 2), 0, keepdims=False)
    ends = jnp.stack([own, end_rows[SLABS_HERE - 1]], 0)
    pairs, count = pair_lists(ends, n_ctx * rows // BLOCK)
    context_head, stats = attend(received, ends, pairs, count)
    context_head, grads_in = lax.optimization_barrier((context_head, grads_in))
    context = lax.all_to_all(context_head, "ctx", split_axis=0, concat_axis=0, tiled=True)

    def by_source(table):
        return jnp.swapaxes(table.reshape(HALF, n_ctx, rows), 0, 1)

    results = attend_back(
        received,
        grads_in,
        context_head,
        stats,
        ends,
        pairs,
        count,
        by_source(cos_all),
        by_source(sin_all),
    )
    back_home = lax.all_to_all(results, "ctx", split_axis=0, concat_axis=0, tiled=True)
    last = (((1,), (1,)), ((), ()))

    context = from_units(context)
    context_other = lax.ppermute(context, "core", swap)
    partial_out = lax.dot_general(
        grad_out_both,
        jnp.concatenate([context, context_other], 1),
        last,
        preferred_element_type=f32,
    ).astype(bf16)

    branch = lax.dot_general(context, weights[:, qkv:], over, preferred_element_type=f32)
    branch = branch.astype(bf16)
    here = jnp.arange(slabs, dtype=jnp.int32)
    marks = (
        (end_rows[:, :, None, None] == first + jnp.arange(rows, dtype=jnp.int32))
        & (here[:, None, None, None] == here[:, None])
    ).astype(bf16)
    marks = marks.reshape(slabs * docs, tok)
    picked = jnp.dot(marks, flat, preferred_element_type=f32) + jnp.dot(
        marks, branch, preferred_element_type=f32
    )
    picked = picked * lax.rsqrt(jnp.mean(picked * picked, -1, keepdims=True) + eps)
    rewards = jnp.sum(picked * head_weight, -1).reshape(slabs, docs)
    hd = HEAD_DIM
    back_home, partial_out = lax.optimization_barrier((back_home, partial_out))
    pieces_out = lax.all_to_all(partial_out, "ctx", split_axis=0, concat_axis=0, tiled=True)
    edge = UNITS * hd
    dquery = from_units(back_home[:, :edge])
    dkey = from_sets(back_home[:, edge : edge + SETS * hd])
    dvalue = from_sets(back_home[:, edge + SETS * hd :])
    grads = jnp.concatenate([dquery, dkey, dvalue], 0)
    partial = lax.dot_general(normed_rows, grads, last, preferred_element_type=f32).astype(bf16)
    partial, grads, context = lax.optimization_barrier((partial, grads, context))
    summed = lax.psum_scatter(partial, ("x", "core"), scatter_dimension=0, tiled=True)
    summed, pieces_out = lax.optimization_barrier((summed, pieces_out))
    sums_out = jnp.sum(pieces_out.reshape(n_ctx, n_x, -1, width).astype(f32), 0)
    place = lax.axis_index("x")
    summed_out = lax.dynamic_index_in_dim(sums_out, place, 0, keepdims=False)
    for shift in range(1, n_x):
        target = lax.rem(place + shift, n_x)
        piece = lax.dynamic_index_in_dim(sums_out, target, 0, keepdims=False)
        around = [(c, (c + shift) % n_x) for c in range(n_x)]
        summed_out = summed_out + lax.ppermute(piece, "x", around)
    parts = []
    rest = rewards.reshape(-1)
    for _ in range(3):
        part = lax.reduce_precision(rest, 8, 7)
        parts.append(part)
        rest = rest - part
    riders = jnp.stack(parts, 0).astype(bf16)
    extra = 128
    riders = jnp.pad(riders, ((0, 16 - len(parts)), (0, extra - riders.shape[1])))
    summed = jnp.concatenate([summed, jnp.tile(riders, (n_ctx, 1))], 1)
    pieces = lax.all_to_all(summed, "ctx", split_axis=0, concat_axis=0, tiled=True)
    dnormed = lax.dot_general(grads, weights[:, :qkv], over, preferred_element_type=f32)
    scaled = dnormed * input_norm_gain
    centered = wide * inverse_norm
    grad_tokens = inverse_norm * (
        scaled - centered * jnp.mean(scaled * centered, -1, keepdims=True)
    )
    pieces = pieces.reshape(n_ctx, -1, qkv + extra)
    summed = jnp.sum(pieces[:, :, :qkv].astype(f32), 0)
    riders = pieces[:, : len(parts), qkv:]
    rewards = jnp.sum(riders[:, :, : slabs * docs].astype(f32), (0, 1)).reshape(slabs, docs)
    return (
        branch.reshape(tokens.shape),
        rewards,
        grad_tokens.astype(bf16).reshape(tokens.shape),
        summed[:, :width],
        summed[:, width : width + kv_width],
        summed[:, width + kv_width :],
        summed_out,
    )


def solution(mesh):
    n_ctx, n_fsdp = mesh.devices.shape
    chips = Mesh(mesh.devices.reshape(n_ctx, n_fsdp // 2, 2), ("ctx", "x", "core"))
    fsdp = ("x", "core")
    rows = P(("ctx", "x", "core"), None)
    acts = P(fsdp, "ctx", None)
    return jax.shard_map(
        on_device,
        mesh=chips,
        in_specs=(
            acts,
            P(fsdp, None),
            P(fsdp, None),
            P(),
            rows,
            rows,
            rows,
            rows,
            P(),
            acts,
        ),
        out_specs=(acts, P(fsdp, None), acts, rows, rows, rows, rows),
        check_vma=False,
    )
```

```python
import jax
import jax.numpy as jnp
from jax import lax
from jax.experimental import pallas as pl
from jax.experimental.pallas import tpu as pltpu
from jax.sharding import Mesh
from jax.sharding import PartitionSpec as P

HEADS = 16
KV_HEADS = 4
HEAD_DIM = 64
GROUP = HEADS // KV_HEADS
SLABS_HERE = 3
SET_OF = (0, 0, 1)
UNITS, SETS = 3, 2
STEPS, BACK_STEPS = 2, 1
HALF = HEAD_DIM // 2
BLOCK = 256

eps = 1e-05
base_theta = 500000.0


def rotation_tables(positions):
    freqs = base_theta ** (-(2.0 * jnp.arange(HALF, dtype=jnp.float32)) / HEAD_DIM)
    angles = positions.astype(jnp.float32)[None, :] * freqs[:, None]
    return jnp.cos(angles), jnp.sin(angles)


def pair_lists(end_rows, blocks, steps):
    at = jnp.arange(blocks, dtype=jnp.int32) * BLOCK
    after = end_rows[:, None, :] + 1
    first = jnp.max(jnp.where(after <= at[None, :, None], after, 0), -1) // BLOCK
    codes = [(i, i - d) for d in range(1, blocks) for i in range(d, blocks)]
    query = jnp.array([i for i, _ in codes], jnp.int32)
    key = jnp.array([j for _, j in codes], jnp.int32)
    lowest = jnp.stack([first[:, i] for i, _ in codes], 1)
    valid = key[None] >= lowest
    places, total = [], jnp.zeros((end_rows.shape[0], 1), jnp.int32)
    at = 0
    for d in range(1, blocks):
        here = valid[:, at : at + blocks - d].astype(jnp.int32)
        places.append(total + jnp.cumsum(here, 1) - 1)
        number = jnp.sum(here, 1, keepdims=True)
        total = total + (number + steps - 1) // steps * steps
        at += blocks - d
    place = jnp.concatenate(places, 1)
    slot = jnp.arange(len(codes) + steps * blocks, dtype=jnp.int32)
    chosen = valid[:, :, None] & (place[:, :, None] == slot)
    code = (query * blocks + key)[None, :, None]
    filled = jnp.any(chosen, 1)
    listed = jnp.where(filled, jnp.sum(jnp.where(chosen, code, 0), 1), blocks - 1)
    return listed, (jnp.max(total) // steps).reshape(1)


def block_of(ref, part, b):
    per = BLOCK // ref.shape[2]
    at = slice(part * HEAD_DIM, (part + 1) * HEAD_DIM)
    return jnp.concatenate([ref[b * per + r, at, :] for r in range(per)], axis=1)


def mask_of(starts, i, j):
    place = lax.broadcasted_iota(jnp.int32, (1, BLOCK), 1) + i * BLOCK
    key = lax.broadcasted_iota(jnp.int32, (BLOCK, BLOCK), 0) + j * BLOCK
    return (key >= starts) & (key <= place)


def starts_of(ends_ref, slab, b):
    place = lax.broadcasted_iota(jnp.int32, (1, BLOCK), 1) + b * BLOCK
    start = jnp.zeros((1, BLOCK), jnp.int32)
    for d in range(ends_ref.shape[1] - 1):
        after = ends_ref[slab, d] + 1
        start = jnp.where(place >= after, after, start)
    return start


def forward_kernel(
    ends_ref, pairs_ref, count_ref, in_ref, out_ref, stats_ref, q_s, k_s, vt_s, start_s, top_s, sum_s, acc_s
):
    n_src, _, rows = in_ref.shape
    per = BLOCK // rows
    blocks = n_src // per
    f32, bf16 = jnp.float32, jnp.bfloat16

    for b in range(blocks):
        for u in range(UNITS):
            q_s[u * blocks + b] = block_of(in_ref, u, b)
        for t in range(SETS):
            at = t * blocks + b
            k_s[at] = block_of(in_ref, UNITS + t, b).T
            vt_s[at] = block_of(in_ref, UNITS + SETS + t, b)
            start_s[at] = starts_of(ends_ref, t, b)

    def scores(u, i, j, mask):
        keys = k_s[SET_OF[u] * blocks + j]
        raw = jnp.dot(keys, q_s[u * blocks + i], preferred_element_type=f32)
        return jnp.where(mask, raw, -jnp.inf)

    def weighted(w, at):
        over_keys = (((0,), (1,)), ((), ()))
        return lax.dot_general(
            w.astype(bf16), vt_s[at], over_keys, preferred_element_type=f32
        ).T

    def diagonal(i, _):
        masks = [mask_of(start_s[t * blocks + i], i, i) for t in range(SETS)]
        done = []
        for u in range(UNITS):
            t = SET_OF[u]
            raw = scores(u, i, i, masks[t])
            top = jnp.max(raw, axis=0, keepdims=True)
            w = jnp.exp(raw - top)
            total = jnp.sum(w, axis=0, keepdims=True)
            done.append((u * blocks + i, top, total, weighted(w, t * blocks + i)))
        for at, top, total, acc in done:
            top_s[at], sum_s[at], acc_s[at] = top, total, acc
        return 0

    lax.fori_loop(0, blocks, diagonal, 0, unroll=True)

    def below(step, _):
        done = []
        for n in range(STEPS * UNITS):
            u = n % UNITS
            t = SET_OF[u]
            if u == 0:
                codes = [pairs_ref[t, step * STEPS + n // UNITS] for t in range(SETS)]
                places = [(lax.div(code, blocks), lax.rem(code, blocks)) for code in codes]
                masks = [mask_of(start_s[t * blocks + i], i, j) for t, (i, j) in enumerate(places)]
            i, j = places[t]
            at = u * blocks + i
            raw = scores(u, i, j, masks[t])
            old = top_s[at]
            top = jnp.maximum(old, jnp.max(raw, axis=0, keepdims=True))
            fade = jnp.exp(old - top)
            w = jnp.exp(raw - top)
            total = sum_s[at] * fade + jnp.sum(w, axis=0, keepdims=True)
            acc = acc_s[at] * fade + weighted(w, t * blocks + j)
            done.append((at, top, total, acc))
        for at, top, total, acc in done:
            top_s[at], sum_s[at], acc_s[at] = top, total, acc
        return 0

    lax.fori_loop(0, count_ref[0], below, 0)

    for u in range(UNITS):
        for b in range(blocks):
            at = u * blocks + b
            inv = 1.0 / sum_s[at]
            stats_ref[at, 0:1, :] = top_s[at]
            stats_ref[at, 1:2, :] = inv
            ctx = (acc_s[at] * inv).astype(bf16)
            for r in range(per):
                out_ref[b * per + r, u * HEAD_DIM : (u + 1) * HEAD_DIM, :] = ctx[
                    :, r * rows : (r + 1) * rows
                ]


def backward_kernel(
    ends_ref,
    pairs_ref,
    count_ref,
    in_ref,
    grad_ref,
    ctx_ref,
    stats_ref,
    cos_ref,
    sin_ref,
    out_ref,
    q_s,
    kt_s,
    k_s,
    v_s,
    g_s,
    start_s,
    delta_s,
    dq_s,
    dk_s,
    dv_s,
):
    n_src, _, rows = in_ref.shape
    per = BLOCK // rows
    blocks = n_src // per
    f32, bf16 = jnp.float32, jnp.bfloat16
    hd = HEAD_DIM

    for b in range(blocks):
        for u in range(UNITS):
            at = u * blocks + b
            grad = block_of(grad_ref, u, b)
            ctx = block_of(ctx_ref, u, b)
            q_s[at] = block_of(in_ref, u, b)
            g_s[at] = grad
            delta_s[at] = jnp.sum(grad.astype(f32) * ctx.astype(f32), axis=0, keepdims=True)
        for t in range(SETS):
            at = t * blocks + b
            kt = block_of(in_ref, UNITS + t, b)
            kt_s[at] = kt
            k_s[at] = kt.T
            v_s[at] = block_of(in_ref, UNITS + SETS + t, b).T
            start_s[at] = starts_of(ends_ref, t, b)

    trans = (((1,), (1,)), ((), ()))

    def terms(places):
        masks = [mask_of(start_s[t * blocks + i], i, j) for t, (i, j) in enumerate(places)]
        dqs, dks, dvs = [], [None] * SETS, [None] * SETS
        for u in range(UNITS):
            t = SET_OF[u]
            i, j = places[t]
            qi, kj = u * blocks + i, t * blocks + j
            query, grad = q_s[qi], g_s[qi]
            raw = jnp.dot(k_s[kj], query, preferred_element_type=f32)
            raw = jnp.where(masks[t], raw, -jnp.inf)
            probs = jnp.exp(raw - stats_ref[qi, 0:1, :]) * stats_ref[qi, 1:2, :]
            dp = jnp.dot(v_s[kj], grad, preferred_element_type=f32)
            ds = (probs * (dp - delta_s[qi])).astype(bf16)
            dv = lax.dot_general(grad, probs.astype(bf16), trans, preferred_element_type=f32)
            dk = lax.dot_general(query, ds, trans, preferred_element_type=f32)
            dqs.append((qi, jnp.dot(kt_s[kj], ds, preferred_element_type=f32)))
            dks[t] = (kj, dk if dks[t] is None else dks[t][1] + dk)
            dvs[t] = (kj, dv if dvs[t] is None else dvs[t][1] + dv)
        return ((dq_s, dqs), (dk_s, dks), (dv_s, dvs))

    def diagonal(i, _):
        for ref, values in terms([(i, i)] * SETS):
            for at, value in values:
                ref[at] = value
        return 0

    lax.fori_loop(0, blocks, diagonal, 0, unroll=True)

    def below(step, _):
        done = []
        for n in range(BACK_STEPS):
            codes = [pairs_ref[t, step * BACK_STEPS + n] for t in range(SETS)]
            places = [(lax.div(code, blocks), lax.rem(code, blocks)) for code in codes]
            done += [
                (ref, at, ref[at] + value) for ref, values in terms(places) for at, value in values
            ]
        for ref, at, value in done:
            ref[at] = value
        return 0

    lax.fori_loop(0, count_ref[0], below, 0)

    def turned_back(grads, at, lanes, src, factor):
        x, y = grads[at, :HALF, lanes] * factor, grads[at, HALF:, lanes] * factor
        cosine, sine = cos_ref[src], sin_ref[src]
        return (x * cosine + y * sine).astype(bf16), (y * cosine - x * sine).astype(bf16)

    for b in range(blocks):
        for r in range(per):
            lanes, src = slice(r * rows, (r + 1) * rows), b * per + r
            for u in range(UNITS):
                x, y = turned_back(dq_s, u * blocks + b, lanes, src, hd**-0.5)
                out_ref[src, u * hd : u * hd + HALF, :] = x
                out_ref[src, u * hd + HALF : (u + 1) * hd, :] = y
            for t in range(SETS):
                at, to = t * blocks + b, UNITS + t
                x, y = turned_back(dk_s, at, lanes, src, 1.0)
                out_ref[src, to * hd : to * hd + HALF, :] = x
                out_ref[src, to * hd + HALF : (to + 1) * hd, :] = y
                to += SETS
                out_ref[src, to * hd : (to + 1) * hd, :] = dv_s[at, :, lanes].astype(bf16)


SMEM = pl.BlockSpec(memory_space=pltpu.SMEM)
VMEM = pl.BlockSpec(memory_space=pltpu.VMEM)
VMEM_LIMIT = 48 * 1024 * 1024


def attend(received, ends, pairs, count):
    n_src, _, rows = received.shape
    blocks = n_src * rows // BLOCK
    n, m = UNITS * blocks, SETS * blocks
    bf16, f32 = jnp.bfloat16, jnp.float32
    row = pltpu.VMEM((n, 1, BLOCK), f32)
    return pl.pallas_call(
        forward_kernel,
        out_shape=(
            jax.ShapeDtypeStruct((n_src, UNITS * HEAD_DIM, rows), bf16),
            jax.ShapeDtypeStruct((n, 2, BLOCK), f32),
        ),
        in_specs=[SMEM, SMEM, SMEM, VMEM],
        out_specs=(VMEM, VMEM),
        scratch_shapes=[
            pltpu.VMEM((n, HEAD_DIM, BLOCK), bf16),
            pltpu.VMEM((m, BLOCK, HEAD_DIM), bf16),
            pltpu.VMEM((m, HEAD_DIM, BLOCK), bf16),
            pltpu.VMEM((m, 1, BLOCK), jnp.int32),
            row,
            row,
            pltpu.VMEM((n, HEAD_DIM, BLOCK), f32),
        ],
        compiler_params=pltpu.CompilerParams(vmem_limit_bytes=VMEM_LIMIT),
        cost_estimate=pl.CostEstimate(
            flops=8 * 10**9, bytes_accessed=4 * 2**20, transcendentals=3 * 2**20
        ),
        name="attend",
    )(ends, pairs, count, received)


def attend_back(received, grads, context, stats, ends, pairs, count, cos_all, sin_all):
    n_src, _, rows = received.shape
    blocks = n_src * rows // BLOCK
    n, m = UNITS * blocks, SETS * blocks
    bf16, f32 = jnp.bfloat16, jnp.float32
    tall = pltpu.VMEM((m, BLOCK, HEAD_DIM), bf16)
    return pl.pallas_call(
        backward_kernel,
        out_shape=jax.ShapeDtypeStruct(received.shape, bf16),
        in_specs=[SMEM, SMEM, SMEM] + [VMEM] * 6,
        out_specs=VMEM,
        scratch_shapes=[
            pltpu.VMEM((n, HEAD_DIM, BLOCK), bf16),
            pltpu.VMEM((m, HEAD_DIM, BLOCK), bf16),
            tall,
            tall,
            pltpu.VMEM((n, HEAD_DIM, BLOCK), bf16),
            pltpu.VMEM((m, 1, BLOCK), jnp.int32),
            pltpu.VMEM((n, 1, BLOCK), f32),
            pltpu.VMEM((n, HEAD_DIM, BLOCK), f32),
            pltpu.VMEM((m, HEAD_DIM, BLOCK), f32),
            pltpu.VMEM((m, HEAD_DIM, BLOCK), f32),
        ],
        compiler_params=pltpu.CompilerParams(vmem_limit_bytes=VMEM_LIMIT),
        cost_estimate=pl.CostEstimate(
            flops=16 * 10**9, bytes_accessed=8 * 2**20, transcendentals=3 * 2**20
        ),
        name="attend_back",
    )(ends, pairs, count, received, grads, context, stats, cos_all, sin_all)


def to_units(heads):
    pairs = heads.reshape(HEADS // 2, 2, HEAD_DIM, -1)
    first, second, last = jnp.split(pairs, SLABS_HERE, axis=-1)
    return jnp.stack(
        [
            jnp.concatenate([own[:, 0], own[:, 1], last[:, e]], 1)
            for e, own in enumerate((first, second))
        ],
        1,
    )


def to_sets(heads):
    first, second, last = jnp.split(heads, SLABS_HERE, axis=-1)
    both = jnp.stack([jnp.concatenate([own, last], 1) for own in (first, second)], 1)
    return jnp.repeat(both, GROUP // 2, axis=0)


def from_units(units):
    rows = units.shape[-1]
    units = units.reshape(HEADS // 2, 2, UNITS, HEAD_DIM, rows)
    parts = [units[:, 0, :2], units[:, 1, :2], units[:, :, 2]]
    return jnp.concatenate(parts, -1).reshape(HEADS * HEAD_DIM, -1)


def from_sets(sets):
    rows = sets.shape[-1]
    sets = sets.astype(jnp.float32)
    sets = sets.reshape(KV_HEADS, GROUP // 2, 2, SETS, HEAD_DIM, rows)
    parts = [
        jnp.sum(sets[:, :, 0, 0], 1),
        jnp.sum(sets[:, :, 1, 0], 1),
        jnp.sum(sets[:, :, :, 1], (1, 2)),
    ]
    return jnp.concatenate(parts, -1).astype(jnp.bfloat16).reshape(KV_HEADS * HEAD_DIM, -1)


def on_device(
    tokens,
    segment_ids,
    end_rows,
    input_norm_gain,
    query_weight,
    key_weight,
    value_weight,
    out_weight,
    head_weight,
    branch_grad,
):
    del segment_ids
    bf16, f32 = jnp.bfloat16, jnp.float32
    n_ctx, n_x, n_core = (lax.axis_size(a) for a in ("ctx", "x", "core"))
    rank = lax.axis_index("ctx")
    core = lax.axis_index("core")
    slabs, rows, model = tokens.shape
    docs = end_rows.shape[1]
    tok = slabs * rows
    width = HEADS * HEAD_DIM
    kv_width = KV_HEADS * HEAD_DIM
    qkv = width + 2 * kv_width
    swap = [(c, n_core - 1 - c) for c in range(n_core)]

    weights = lax.all_gather(
        jnp.concatenate([query_weight, key_weight, value_weight, out_weight], 1),
        ("ctx", "x", "core"),
        axis=0,
        tiled=True,
    )

    flat = tokens.reshape(tok, model)
    grad_out = branch_grad.reshape(tok, model)
    wide = flat.astype(f32)
    inverse_norm = lax.rsqrt(jnp.mean(wide * wide, -1, keepdims=True) + eps)
    normed = (wide * inverse_norm * input_norm_gain).astype(bf16)

    split = grad_out.T.reshape(model // (16 * n_core), n_core, 16, tok)
    mine = lax.dynamic_index_in_dim(split, core, 1, keepdims=False).reshape(-1, tok)
    other = lax.dynamic_index_in_dim(split, 1 - core, 1, keepdims=False).reshape(-1, tok)
    grad_out_both = jnp.concatenate([mine, lax.ppermute(other, "core", swap)], 1)
    n_fsdp = n_x * n_core
    normed_rows = jnp.swapaxes(normed.T.reshape(n_ctx, n_fsdp, 16, tok), 0, 1)
    normed_rows = normed_rows.reshape(model, tok)

    first = rank * rows
    cos_all, sin_all = rotation_tables(jnp.arange(n_ctx * rows, dtype=jnp.int32))
    cos_here, sin_here = rotation_tables(first + jnp.arange(rows, dtype=jnp.int32))
    cos_here = jnp.tile(cos_here, (1, slabs))[None]
    sin_here = jnp.tile(sin_here, (1, slabs))[None]
    over = (((0,), (1,)), ((), ()))
    projected = lax.dot_general(weights[:, :qkv], normed, over, preferred_element_type=f32)
    turning = projected[: width + kv_width].reshape(HEADS + KV_HEADS, 2, HALF, tok)
    front, back = turning[:, 0], turning[:, 1]
    turned = jnp.concatenate(
        [front * cos_here - back * sin_here, back * cos_here + front * sin_here], 1
    )
    query = (turned[:HEADS] * (HEAD_DIM**-0.5)).astype(bf16)
    keys = turned[HEADS:].astype(bf16)
    values = projected[width + kv_width :].astype(bf16).reshape(KV_HEADS, HEAD_DIM, tok)
    send = jnp.concatenate([to_units(query), to_sets(keys), to_sets(values)], 2)
    send = send.reshape(HEADS, -1, rows)
    received = lax.all_to_all(send, "ctx", split_axis=0, concat_axis=0, tiled=True)
    context_grad = lax.dot_general(
        weights[:, qkv:], grad_out, over, preferred_element_type=f32
    ).astype(bf16)
    grads_in = lax.all_to_all(
        to_units(context_grad).reshape(HEADS, -1, rows), "ctx", split_axis=0, concat_axis=0, tiled=True
    )

    own = lax.dynamic_index_in_dim(end_rows, lax.rem(rank, 2), 0, keepdims=False)
    ends = jnp.stack([own, end_rows[SLABS_HERE - 1]], 0)
    blocks = n_ctx * rows // BLOCK
    pairs, count = pair_lists(ends, blocks, STEPS)
    back_pairs, back_count = pair_lists(ends, blocks, BACK_STEPS)
    context_head, stats = attend(received, ends, pairs, count)
    context_head, grads_in = lax.optimization_barrier((context_head, grads_in))
    context = lax.all_to_all(context_head, "ctx", split_axis=0, concat_axis=0, tiled=True)

    def by_source(table):
        return jnp.swapaxes(table.reshape(HALF, n_ctx, rows), 0, 1)

    results = attend_back(
        received,
        grads_in,
        context_head,
        stats,
        ends,
        back_pairs,
        back_count,
        by_source(cos_all),
        by_source(sin_all),
    )
    back_home = lax.all_to_all(results, "ctx", split_axis=0, concat_axis=0, tiled=True)
    last = (((1,), (1,)), ((), ()))

    context = from_units(context)
    context_other = lax.ppermute(context, "core", swap)
    partial_out = lax.dot_general(
        grad_out_both,
        jnp.concatenate([context, context_other], 1),
        last,
        preferred_element_type=f32,
    ).astype(bf16)

    branch = lax.dot_general(context, weights[:, qkv:], over, preferred_element_type=f32)
    branch = branch.astype(bf16)
    here = jnp.arange(slabs, dtype=jnp.int32)
    marks = (
        (end_rows[:, :, None, None] == first + jnp.arange(rows, dtype=jnp.int32))
        & (here[:, None, None, None] == here[:, None])
    ).astype(bf16)
    marks = marks.reshape(slabs * docs, tok)
    picked = jnp.dot(marks, flat, preferred_element_type=f32) + jnp.dot(
        marks, branch, preferred_element_type=f32
    )
    picked = picked * lax.rsqrt(jnp.mean(picked * picked, -1, keepdims=True) + eps)
    rewards = jnp.sum(picked * head_weight, -1).reshape(slabs, docs)
    hd = HEAD_DIM
    back_home, partial_out = lax.optimization_barrier((back_home, partial_out))
    pieces_out = lax.all_to_all(partial_out, "ctx", split_axis=0, concat_axis=0, tiled=True)
    edge = UNITS * hd
    dquery = from_units(back_home[:, :edge])
    dkey = from_sets(back_home[:, edge : edge + SETS * hd])
    dvalue = from_sets(back_home[:, edge + SETS * hd :])
    grads = jnp.concatenate([dquery, dkey, dvalue], 0)
    partial = lax.dot_general(normed_rows, grads, last, preferred_element_type=f32).astype(bf16)
    partial, grads, context = lax.optimization_barrier((partial, grads, context))
    summed = lax.psum_scatter(partial, ("x", "core"), scatter_dimension=0, tiled=True)
    summed, pieces_out = lax.optimization_barrier((summed, pieces_out))
    sums_out = jnp.sum(pieces_out.reshape(n_ctx, n_x, -1, width).astype(f32), 0)
    place = lax.axis_index("x")
    summed_out = lax.dynamic_index_in_dim(sums_out, place, 0, keepdims=False)
    for shift in range(1, n_x):
        target = lax.rem(place + shift, n_x)
        piece = lax.dynamic_index_in_dim(sums_out, target, 0, keepdims=False)
        around = [(c, (c + shift) % n_x) for c in range(n_x)]
        summed_out = summed_out + lax.ppermute(piece, "x", around)
    parts = []
    rest = rewards.reshape(-1)
    for _ in range(3):
        part = lax.reduce_precision(rest, 8, 7)
        parts.append(part)
        rest = rest - part
    riders = jnp.stack(parts, 0).astype(bf16)
    extra = 128
    riders = jnp.pad(riders, ((0, 16 - len(parts)), (0, extra - riders.shape[1])))
    summed = jnp.concatenate([summed, jnp.tile(riders, (n_ctx, 1))], 1)
    pieces = lax.all_to_all(summed, "ctx", split_axis=0, concat_axis=0, tiled=True)
    dnormed = lax.dot_general(grads, weights[:, :qkv], over, preferred_element_type=f32)
    scaled = dnormed * input_norm_gain
    centered = wide * inverse_norm
    grad_tokens = inverse_norm * (
        scaled - centered * jnp.mean(scaled * centered, -1, keepdims=True)
    )
    pieces = pieces.reshape(n_ctx, -1, qkv + extra)
    summed = jnp.sum(pieces[:, :, :qkv].astype(f32), 0)
    riders = pieces[:, : len(parts), qkv:]
    rewards = jnp.sum(riders[:, :, : slabs * docs].astype(f32), (0, 1)).reshape(slabs, docs)
    return (
        branch.reshape(tokens.shape),
        rewards,
        grad_tokens.astype(bf16).reshape(tokens.shape),
        summed[:, :width],
        summed[:, width : width + kv_width],
        summed[:, width + kv_width :],
        summed_out,
    )


def solution(mesh):
    n_ctx, n_fsdp = mesh.devices.shape
    chips = Mesh(mesh.devices.reshape(n_ctx, n_fsdp // 2, 2), ("ctx", "x", "core"))
    fsdp = ("x", "core")
    rows = P(("ctx", "x", "core"), None)
    acts = P(fsdp, "ctx", None)
    return jax.shard_map(
        on_device,
        mesh=chips,
        in_specs=(
            acts,
            P(fsdp, None),
            P(fsdp, None),
            P(),
            rows,
            rows,
            rows,
            rows,
            P(),
            acts,
        ),
        out_specs=(acts, P(fsdp, None), acts, rows, rows, rows, rows),
        check_vma=False,
    )
```
